32 devices in a mesh: comp: 4 (over y, core), horiz: 2 (over x), trc: 4 (over z).
Axes of the slice: x: 2, y: 2, z: 4, core: 2. Of those that a mesh axis runs over, the one named last changes fastest.
Arguments:
- tracers: float32 [16, 64, 64, 256], P(('comp', 'trc'), None, 'horiz'), may hold values from -6 to 6
- eastward: float32 [64, 64, 256], P(('comp', 'trc'), 'horiz'), may hold values from -1.2 to 1.2
- northward: float32 [64, 64, 256], P(('comp', 'trc'), 'horiz'), may hold values from -1.2 to 1.2
- surface_height: float32 [64, 256], P('horiz'), may hold values from -6 to 6
- sea_mask: int32 [64, 256], P('horiz'), may hold values 0 or 1
- mixing: float32 [64, 64, 256], P(('comp', 'trc'), 'horiz'), may hold values from 0.02 to 0.15
- sunlight: float32 [64, 256], P('horiz'), may hold values from 0.5 to 4
- reaction: float32 [16, 16], replicated, may hold values from -1.5 to 1.5
Outputs:
- east_out: float32 [64, 64, 256], P(('comp', 'trc'), 'horiz')
- north_out: float32 [64, 64, 256], P(('comp', 'trc'), 'horiz')
- tracers_out: float32 [16, 64, 64, 256], P(None, ('comp', 'trc'), 'horiz')
- heating: float32 [64, 64, 256], P(('comp', 'trc'), 'horiz')
The draws below stay inside these ranges and needn't reach their ends.
All inputs are finite; a program needn't handle non-finite values. No bound on the sum of `sea_mask` on one device may be relied on, other than what follows from the above.
Results may differ from the reference program's by a relative error of at most 0.00017.
Values sent between devices are 32-bit elements; how exact they have to be, the bound alone decides.
A program may use at most 64 MiB of HBM per device.

```python
import math
import jax
import jax.numpy as jnp
from jax import lax

NTR = 16
Y = 256
SUBSTEPS = 4
X = 64
LEVELS = 64


def set_ends(values, rng, least, largest):
    longest = values.shape.index(max(values.shape))
    spots = []
    for shift in (0, 1):
        where = [jax.random.randint(jax.random.fold_in(rng, axis), (), 0, length) for axis, length in enumerate(values.shape)]
        where[longest] = (where[longest] + shift) % values.shape[longest]
        spots.append(tuple(where))
    return values.at[spots[0]].set(least).at[spots[1]].set(largest)


def steps_of(stream_key, extent, split, least, high):
    def one(dim, blocks):
        draws = jax.random.uniform(jax.random.fold_in(jax.random.fold_in(stream_key, 6), dim), (blocks,), jnp.float32, least / len(split), high / len(split))
        return jnp.repeat(jnp.exp(draws), extent[dim] // blocks).reshape((-1,) + (1,) * (len(extent) - dim - 1))

    factor_of = one(*split[0])
    for cut in split[1:]:
        factor_of = factor_of * one(*cut)
    return factor_of


def bell_draw(stream_key, shape, deviation, most, shards=(), kind=jnp.bfloat16):
    drawn = jax.random.normal(stream_key, shape, jnp.float32) * deviation
    if len(shards) > 0:
        drawn = steps_of(stream_key, shape, shards, -0.22, 0.18) * drawn
    return jnp.clip(drawn, min=-most, max=most).astype(kind)


def setup_inputs(seed: int = 0) -> dict:
    seeds = jax.random.split(jax.random.key(seed), 9)
    tracers = bell_draw(seeds[0], (NTR, LEVELS, X, Y), 1.0, 6.0, ((0, 16), (2, 2)), jnp.float32)
    eastward = bell_draw(seeds[1], (LEVELS, X, Y), 0.4, 1.2, ((0, 16), (1, 2)), jnp.float32)
    northward = bell_draw(seeds[2], (LEVELS, X, Y), 0.4, 1.2, ((0, 16), (1, 2)), jnp.float32)
    surface_height = bell_draw(seeds[3], (X, Y), 1.0, 6.0, ((0, 2),), jnp.float32)
    sea_mask = set_ends((jax.random.randint(seeds[4], (X, Y), 0, 5) < 4).astype(jnp.int32), jax.random.fold_in(seeds[4], 1), 0, 1)
    mixing = jnp.clip(jnp.exp(math.log(0.15) - 2.014903 * jax.random.uniform(seeds[5], (LEVELS, X, Y), jnp.float32) ** steps_of(seeds[5], (LEVELS, X, Y), ((0, 16), (1, 2)), -0.2, 0.2)), 0.02, 0.15)
    sunlight = jnp.clip(jnp.exp(math.log(4.0) - 2.0794415 * jax.random.uniform(seeds[6], (X, Y), jnp.float32) ** steps_of(seeds[6], (X, Y), ((0, 2),), -0.2, 0.2)), 0.5, 4.0)
    reaction = bell_draw(seeds[7], (NTR, NTR), NTR ** -0.5, 1.5, (), jnp.float32)
    return dict(tracers=tracers, eastward=eastward, northward=northward, surface_height=surface_height, sea_mask=sea_mask, mixing=mixing, sunlight=sunlight, reaction=reaction)


TIME_STEP = 0.25
GRAVITY = 1.0
VISCOSITY = 0.05
COURANT = 0.2
HALF_LIGHT = 0.3


def pad_rows(array):
    return jnp.pad(array, [(0, 0)] * (array.ndim - 1) + [(1, 1)])


def ocean_step(east_ext, north_ext, height_ext, wet_ext, mixing, bottom_keep):
    width = east_ext.shape[1] - 4
    rows = east_ext.shape[2]
    coriolis = 0.5 + 0.5 * jnp.arange(rows, dtype=jnp.float32) / rows
    east_pad = pad_rows(east_ext)
    north_pad = pad_rows(north_ext)
    height_pad = pad_rows(height_ext)
    wet_pad = pad_rows(wet_ext)
    east_mid = east_ext[:, 1:width + 2]
    east_lap = (east_ext[:, 2:width + 3] + east_ext[:, 0:width + 1] + east_pad[:, 1:width + 2, 2:]
                + east_pad[:, 1:width + 2, :-2] - 4.0 * east_mid)
    north_avg = 0.25 * (north_pad[:, 1:width + 2, 1:-1] + north_pad[:, 2:width + 3, 1:-1]
                        + north_pad[:, 1:width + 2, :-2] + north_pad[:, 2:width + 3, :-2])
    slope_x = height_ext[2:width + 3] - height_ext[1:width + 2]
    open_x = wet_ext[1:width + 2] * wet_ext[2:width + 3]
    east_new = open_x * (east_mid + TIME_STEP * (coriolis * north_avg - GRAVITY * slope_x + VISCOSITY * east_lap))
    north_mid = north_ext[:, 2:width + 2]
    north_lap = (north_ext[:, 3:width + 3] + north_ext[:, 1:width + 1] + north_pad[:, 2:width + 2, 2:]
                 + north_pad[:, 2:width + 2, :-2] - 4.0 * north_mid)
    east_avg = 0.25 * (east_pad[:, 2:width + 2, 1:-1] + east_pad[:, 1:width + 1, 1:-1]
                       + east_pad[:, 2:width + 2, 2:] + east_pad[:, 1:width + 1, 2:])
    slope_y = height_pad[2:width + 2, 2:] - height_pad[2:width + 2, 1:-1]
    open_y = wet_pad[2:width + 2, 1:-1] * wet_pad[2:width + 2, 2:]
    north_new = open_y * (north_mid + TIME_STEP * (-coriolis * east_avg - GRAVITY * slope_y + VISCOSITY * north_lap))
    east_out = east_new[:, 1:]
    speed = jnp.minimum(east_out * east_out + north_new * north_new, 1.0)
    kappa = wet_ext[2:width + 2] * mixing * (1.0 + speed) * bottom_keep
    return east_out, north_new, COURANT * east_new, COURANT * north_new, kappa


def advance(padded, flux_x, flux_y, kappa, kappa_up):
    inner = padded[..., 1:-1, 1:-1, :]
    level_mid = padded[..., 1:-1, :, :]
    width = inner.shape[-2]
    east_flux = (jnp.maximum(flux_x, 0.0) * level_mid[..., 0:width + 1, :]
                 + jnp.minimum(flux_x, 0.0) * level_mid[..., 1:width + 2, :])
    across_x = east_flux[..., :-1, :] - east_flux[..., 1:, :]
    north_cells = jnp.pad(inner[..., 1:], [(0, 0)] * (inner.ndim - 1) + [(0, 1)])
    north_flux = jnp.maximum(flux_y, 0.0) * inner + jnp.minimum(flux_y, 0.0) * north_cells
    south_flux = jnp.pad(north_flux[..., :-1], [(0, 0)] * (inner.ndim - 1) + [(1, 0)])
    across_y = south_flux - north_flux
    below = kappa * (padded[..., 2:, 1:-1, :] - inner)
    above = kappa_up * (inner - padded[..., :-2, 1:-1, :])
    return inner + across_x + across_y + below - above


def reference(tracers, eastward, northward, surface_height, sea_mask, mixing, sunlight, reaction):
    levels = eastward.shape[0]
    wet = sea_mask.astype(jnp.float32)
    xpad = ((0, 0), (2, 2), (0, 0))
    keep = (jnp.arange(levels) < levels - 1).astype(jnp.float32)[:, None, None]
    east_out, north_out, flux_x, flux_y, kappa = ocean_step(
        jnp.pad(eastward, xpad), jnp.pad(northward, xpad),
        jnp.pad(surface_height, ((2, 2), (0, 0))), jnp.pad(wet, ((2, 2), (0, 0))), mixing, keep)
    kappa_up = jnp.pad(kappa[:-1], ((1, 0), (0, 0), (0, 0)))

    def transport(field):
        for step in range(SUBSTEPS):
            padded = jnp.pad(field, ((1, 1), (1, 1), (0, 0)))
            field = advance(padded, flux_x, flux_y, kappa, kappa_up)
        return field

    moved = lax.map(transport, tracers)
    tau = (0.5 + moved[0] * moved[0]) / levels
    depth_top = jnp.cumsum(tau, 0) - tau
    light_top = sunlight * jnp.exp(-depth_top)
    heating = levels * light_top * (1.0 - jnp.exp(-tau))
    light_mid = light_top * jnp.exp(-0.5 * tau)
    limit = light_mid / (light_mid + HALF_LIGHT)
    growth = jnp.einsum("ij,jlxy->ilxy", reaction, moved, precision=lax.Precision.HIGHEST)
    tracers_out = moved + limit * growth
    return east_out, north_out, tracers_out, heating
```

```python
import functools

import jax
import jax.numpy as jnp
from jax import lax
from jax.experimental import pallas as pl
from jax.experimental.pallas import tpu as pltpu
from jax.sharding import PartitionSpec as P

SUBSTEPS = 4


TIME_STEP = 0.25
GRAVITY = 1.0
VISCOSITY = 0.05
COURANT = 0.2
HALF_LIGHT = 0.3


def with_halo(block, sides, width):
    for axis, dim in sides:
        count = lax.axis_size(axis)
        forward = [(i, i + 1) for i in range(count - 1)]
        backward = [(target, source) for source, target in forward]
        low = lax.ppermute(
            lax.slice_in_dim(block, block.shape[dim] - width, None, axis=dim), axis, forward
        )
        high = lax.ppermute(lax.slice_in_dim(block, 0, width, axis=dim), axis, backward)
        block = jnp.concatenate([low, block, high], axis=dim)
    return block


def pad_rows(array):
    return jnp.pad(array, [(0, 0)] * (array.ndim - 1) + [(1, 1)])


def ocean_step(east_ext, north_ext, height_ext, wet_ext, mixing, bottom_keep):
    width = east_ext.shape[1] - 4
    rows = east_ext.shape[2]
    coriolis = 0.5 + 0.5 * jnp.arange(rows, dtype=jnp.float32) / rows
    east_pad = pad_rows(east_ext)
    north_pad = pad_rows(north_ext)
    height_pad = pad_rows(height_ext)
    wet_pad = pad_rows(wet_ext)
    east_mid = east_ext[:, 1 : width + 2]
    east_lap = (
        east_ext[:, 2 : width + 3]
        + east_ext[:, 0 : width + 1]
        + east_pad[:, 1 : width + 2, 2:]
        + east_pad[:, 1 : width + 2, :-2]
        - 4.0 * east_mid
    )
    north_avg = 0.25 * (
        north_pad[:, 1 : width + 2, 1:-1]
        + north_pad[:, 2 : width + 3, 1:-1]
        + north_pad[:, 1 : width + 2, :-2]
        + north_pad[:, 2 : width + 3, :-2]
    )
    slope_x = height_ext[2 : width + 3] - height_ext[1 : width + 2]
    open_x = wet_ext[1 : width + 2] * wet_ext[2 : width + 3]
    east_new = open_x * (
        east_mid + TIME_STEP * (coriolis * north_avg - GRAVITY * slope_x + VISCOSITY * east_lap)
    )
    north_mid = north_ext[:, 2 : width + 2]
    north_lap = (
        north_ext[:, 3 : width + 3]
        + north_ext[:, 1 : width + 1]
        + north_pad[:, 2 : width + 2, 2:]
        + north_pad[:, 2 : width + 2, :-2]
        - 4.0 * north_mid
    )
    east_avg = 0.25 * (
        east_pad[:, 2 : width + 2, 1:-1]
        + east_pad[:, 1 : width + 1, 1:-1]
        + east_pad[:, 2 : width + 2, 2:]
        + east_pad[:, 1 : width + 1, 2:]
    )
    slope_y = height_pad[2 : width + 2, 2:] - height_pad[2 : width + 2, 1:-1]
    open_y = wet_pad[2 : width + 2, 1:-1] * wet_pad[2 : width + 2, 2:]
    north_new = open_y * (
        north_mid + TIME_STEP * (-coriolis * east_avg - GRAVITY * slope_y + VISCOSITY * north_lap)
    )
    east_out = east_new[:, 1:]
    speed = jnp.minimum(east_out * east_out + north_new * north_new, 1.0)
    kappa = wet_ext[2 : width + 2] * mixing * (1.0 + speed) * bottom_keep
    return (east_out, north_new, COURANT * east_new, COURANT * north_new, kappa)


TILE = 8
MESH = pl.DeviceIdType.MESH


def remote(src, dst, send, recv, device):
    return pltpu.make_async_remote_copy(
        src_ref=src, dst_ref=dst, send_sem=send, recv_sem=recv, device_id=device, device_id_type=MESH
    )


def kernel(
    dims, tr, coef, sun, react, out, heat,
    T, side, F, CF, tot, totr, pre, abv,
    ts, tl, trs, cs, cr, ks, kr, hs, hr, zs, zr, us, ur, bs, br,
):
    C, H, Z, levels = dims
    c, h, z = (lax.axis_index(a) for a in ("comp", "horiz", "trc"))
    group = coef.shape[1]
    deep = group * Z
    rows, wide = tr.shape[2], T.shape[3]
    cols = tr.shape[3]
    has_left, has_right = h > 0, h < H - 1

    def greet(device):
        pl.semaphore_signal(pltpu.get_barrier_semaphore(), inc=1, device_id=device, device_id_type=MESH)

    for d in range(C):
        c2 = lax.rem(c + d, C)
        if d:
            greet((c2, h, z))
        pl.when(has_left)(functools.partial(greet, (c2, h - 1, z)))
        pl.when(has_right)(functools.partial(greet, (c2, h + 1, z)))
    for d in range(1, Z):
        greet((c, h, lax.rem(z + d, Z)))
    near = has_left.astype(jnp.int32) + has_right.astype(jnp.int32)
    pl.semaphore_wait(pltpu.get_barrier_semaphore(), C * (1 + near) - 1 + Z - 1)

    def coef_copy(up, block):
        where = pl.ds(1 + block * group, group)
        src = CF.at[:, where]
        return remote(src, CF.at[:, where], cs.at[up, block], cr.at[block], (c, h, z + 1 if up else z - 1))

    CF[:, pl.ds(1 + z * group, group)] = coef[...]
    pl.when(z < Z - 1)(lambda: coef_copy(1, z).start())
    pl.when(z > 0)(lambda: coef_copy(0, z).start())

    def tracer_copies(target, source, partner):
        low, high = int(target > 0), int(target < C - 1)
        count = deep + low + high
        src = pl.ds(target * deep - low, count)
        dst = pl.ds(1 - low, count)
        middle = (tr.at[0, src], T.at[0, source, dst, pl.ds(0, rows)])
        left = remote(
            tr.at[0, src, pl.ds(rows - TILE, TILE)], side.at[0, source, dst],
            ts.at[target, 1], trs.at[source, 1], (partner, h + 1, z))
        right = remote(
            tr.at[0, src, pl.ds(0, TILE)], side.at[1, source, dst],
            ts.at[target, 2], trs.at[source, 2], (partner, h - 1, z))
        here = pltpu.make_async_copy(*middle, tl.at[0])
        there = remote(*middle, ts.at[target, 0], trs.at[source, 0], (partner, h, z))
        return here, there, left, right

    for c2 in range(C):
        here, there, left, right = tracer_copies(c2, c, c2)
        pl.when(c == c2)(here.start)
        pl.when(c != c2)(there.start)
        pl.when(has_right)(left.start)
        pl.when(has_left)(right.start)

    @pl.when(h == 0)
    def _():
        side[0] = jnp.zeros(side.shape[1:], jnp.float32)

    @pl.when(h == H - 1)
    def _():
        side[1] = jnp.zeros(side.shape[1:], jnp.float32)

    @pl.when(c == 0)
    def _():
        CF[2, 0] = jnp.zeros((wide, cols), jnp.float32)
        for s in range(SUBSTEPS):
            for k in range(C):
                T[s, k, 0] = jnp.zeros((wide, cols), jnp.float32)
        for k in range(C):
            side[0, k, 0] = jnp.zeros((TILE, cols), jnp.float32)
            side[1, k, 0] = jnp.zeros((TILE, cols), jnp.float32)

    @pl.when(c == C - 1)
    def _():
        for s in range(SUBSTEPS):
            for k in range(C):
                T[s, k, deep + 1] = jnp.zeros((wide, cols), jnp.float32)
        for k in range(C):
            side[0, k, deep + 1] = jnp.zeros((TILE, cols), jnp.float32)
            side[1, k, deep + 1] = jnp.zeros((TILE, cols), jnp.float32)

    for d in range(1, Z):
        @pl.when(z >= d)
        def _():
            coef_copy(1, z - d).wait_recv()
            pl.when(z < Z - 1)(lambda: coef_copy(1, z - d).start())

        @pl.when(z + d < Z)
        def _():
            coef_copy(0, z + d).wait_recv()
            pl.when(z > 0)(lambda: coef_copy(0, z + d).start())

    kup = remote(CF.at[2, deep], CF.at[2, 0], ks.at[0], kr.at[0], (c + 1, h, z))
    pl.when(c < C - 1)(kup.start)
    pl.when(c > 0)(kup.wait_recv)

    def halo(s, k):
        down = remote(T.at[s, k, deep], T.at[s, k, 0], hs.at[s, k, 0], hr.at[s, k, 0], (c + 1, h, z))
        up = remote(T.at[s, k, 1], T.at[s, k, deep + 1], hs.at[s, k, 1], hr.at[s, k, 1], (c - 1, h, z))
        return down, up

    def deliver(k, target, source):
        return remote(
            T.at[SUBSTEPS, k, pl.ds(1 + target * group, group), pl.ds(0, rows)], F.at[k * Z + source],
            zs.at[k, target], zr.at[k, source], (c, h, target))

    def total_copy(target, source):
        return remote(tot, totr.at[source], us.at[target], ur.at[source], (target, h, z))

    def above_copy(target):
        return remote(pre.at[target], abv, bs.at[target], br.at[0], (c, h, target))

    sub = lax.broadcasted_iota(jnp.int32, (TILE, cols), 0)

    def arrive(k):
        for cc in range(C):
            @pl.when(c == cc)
            def _():
                here, there, left, right = tracer_copies(cc, k, cc)
                pl.when(k == cc)(here.wait)
                pl.when(k != cc)(there.wait_recv)
                pl.when(has_left)(left.wait_recv)
                pl.when(has_right)(right.wait_recv)

        @pl.loop(0, deep + 2)
        def _(l):
            T[0, k, l, pl.ds(rows, TILE)] = jnp.where(sub < TILE // 2, side[1, k, l], side[0, k, l])

    def optics(m):
        return (0.5 + m * m) / levels

    def light_totals():
        run = jnp.zeros((rows, cols), jnp.float32)
        for block in range(Z):
            pre[block] = run
            for l in range(group):
                run = run + optics(T[SUBSTEPS, 0, 1 + block * group + l, pl.ds(0, rows)])
        tot[...] = run
        for c2 in range(1, C):
            pl.when(c < c2)(total_copy(c2, c).start)

    def light_above():
        base = jnp.zeros((rows, cols), jnp.float32)
        abv[...] = base
        for c2 in range(C - 1):
            @pl.when(c > c2)
            def _():
                total_copy(c, c2).wait_recv()
                abv[...] += totr[c2]
        for block in range(1, Z):
            pre[block] = pre[block] + abv[...]
            above_copy(block).start()

    def work(index, carry):
        s, k = index // C, lax.rem(index, C)
        pl.when(s == 0)(functools.partial(arrive, k))

        @pl.when(s > 0)
        def _():
            down, up = halo(s, k)
            pl.when(c > 0)(down.wait_recv)
            pl.when(c < C - 1)(up.wait_recv)

        pl.when((s == SUBSTEPS - 1) & (k == C - 1) & (z == 0))(light_above)

        def level(l, carry):
            up, mid, down = T[s, k, l], T[s, k, l + 1], T[s, k, l + 2]
            fx, fy = CF[0, l + 1], CF[1, l + 1]
            E = jnp.maximum(fx, 0.0) * mid + jnp.minimum(fx, 0.0) * pltpu.roll(mid, wide - 1, 0)
            N = jnp.maximum(fy, 0.0) * mid + jnp.minimum(fy, 0.0) * pltpu.roll(mid, cols - 1, 1)
            T[s + 1, k, l + 1] = (
                mid + (pltpu.roll(E, 1, 0) - E) + (pltpu.roll(N, 1, 1) - N)
                + CF[2, l + 1] * (down - mid) - CF[2, l] * (mid - up)
            )
            return carry

        lax.fori_loop(0, deep, level, 0)

        @pl.when(s < SUBSTEPS - 1)
        def _():
            down, up = halo(s + 1, k)
            pl.when(c < C - 1)(down.start)
            pl.when(c > 0)(up.start)

        @pl.when(s == SUBSTEPS - 1)
        def _():
            for d in range(1, Z):
                deliver(k, lax.rem(z + d, Z), z).start()
            F[k * Z + z] = T[SUBSTEPS, k, pl.ds(1 + z * group, group), pl.ds(0, rows)]
            pl.when((k == 0) & (z == 0))(light_totals)

        return carry

    lax.fori_loop(0, SUBSTEPS * C, work, 0)

    pl.when(z > 0)(above_copy(z).wait_recv)
    for k in range(C):
        for d in range(1, Z):
            deliver(k, z, lax.rem(z + d, Z)).wait_recv()

    def react_tile(index, carry):
        l, r = index // (rows // TILE), lax.rem(index, rows // TILE)
        here = pl.ds(pl.multiple_of(r * TILE, TILE), TILE)
        field = [F[j, l, here] for j in range(F.shape[0])]
        tau = optics(field[0])
        depth = abv[here]
        abv[here] = depth + tau
        light_top = sun[here] * jnp.exp(-depth)
        heat[l, here] = levels * light_top * (1.0 - jnp.exp(-tau))
        light_mid = light_top * jnp.exp(-0.5 * tau)
        limit = light_mid / (light_mid + HALF_LIGHT)
        for i in range(F.shape[0]):
            growth = react[i, 0] * field[0]
            for j in range(1, F.shape[0]):
                growth = growth + react[i, j] * field[j]
            out[i, l, here] = field[i] + limit * growth
        return carry

    lax.fori_loop(0, group * (rows // TILE), react_tile, 0)

    pl.when(z < Z - 1)(lambda: coef_copy(1, z).wait_send())
    pl.when(z > 0)(lambda: coef_copy(0, z).wait_send())
    for d in range(1, Z):
        pl.when((z >= d) & (z < Z - 1))(lambda: coef_copy(1, z - d).wait_send())
        pl.when((z + d < Z) & (z > 0))(lambda: coef_copy(0, z + d).wait_send())
    for c2 in range(C):
        here, there, left, right = tracer_copies(c2, c, c2)
        pl.when(c != c2)(there.wait_send)
        pl.when(has_right)(left.wait_send)
        pl.when(has_left)(right.wait_send)
    pl.when(c < C - 1)(kup.wait_send)
    for s in range(1, SUBSTEPS):
        for k in range(C):
            down, up = halo(s, k)
            pl.when(c < C - 1)(down.wait_send)
            pl.when(c > 0)(up.wait_send)
    for k in range(C):
        for d in range(1, Z):
            deliver(k, lax.rem(z + d, Z), z).wait_send()

    @pl.when(z == 0)
    def _():
        for c2 in range(1, C):
            pl.when(c < c2)(total_copy(c2, c).wait_send)
        for block in range(1, Z):
            above_copy(block).wait_send()


def per_device(dims, tracers, eastward, northward, surface_height, sea_mask, mixing, sunlight, reaction):
    C, H, Z, levels = dims
    group, rows, cols = eastward.shape
    half = TILE // 2
    first_level = lax.axis_index(("comp", "trc")) * group
    keep = (first_level + jnp.arange(group) < levels - 1).astype(jnp.float32)[:, None, None]
    wet = sea_mask.astype(jnp.float32)
    stacked = jnp.concatenate([eastward, northward, mixing, surface_height[None], wet[None]], 0)
    edges = with_halo(stacked, (("horiz", 1),), half + 2)
    east, north, flux_x, flux_y, kappa = ocean_step(
        edges[:group], edges[group : 2 * group], edges[3 * group], edges[3 * group + 1],
        edges[2 * group : 3 * group, 2:-2], keep,
    )
    coef = jnp.stack([flux_x[:, 1:], flux_y, kappa])
    coef = jnp.concatenate([coef[:, :, half:], coef[:, :, :half]], 2)
    wide, deep, f32 = rows + TILE, group * Z, jnp.float32
    dma = pltpu.SemaphoreType.DMA
    vmem = pl.BlockSpec(memory_space=pltpu.VMEM)
    tracers_out, heating = pl.pallas_call(
        functools.partial(kernel, dims),
        out_shape=(
            jax.ShapeDtypeStruct((C * Z, group, rows, cols), f32),
            jax.ShapeDtypeStruct((group, rows, cols), f32),
        ),
        in_specs=[pl.BlockSpec(memory_space=pl.ANY), vmem, vmem, pl.BlockSpec(memory_space=pltpu.SMEM)],
        out_specs=(vmem, vmem),
        scratch_shapes=[
            pltpu.VMEM((SUBSTEPS + 1, C, deep + 2, wide, cols), f32),
            pltpu.VMEM((2, C, deep + 2, TILE, cols), f32),
            pltpu.VMEM((C * Z, group, rows, cols), f32),
            pltpu.VMEM((3, deep + 1, wide, cols), f32),
            pltpu.VMEM((rows, cols), f32),
            pltpu.VMEM((C, rows, cols), f32),
            pltpu.VMEM((Z, rows, cols), f32),
            pltpu.VMEM((rows, cols), f32),
            dma((C, 3)), dma((1,)), dma((C, 3)),
            dma((2, Z)), dma((Z,)),
            dma((1,)), dma((1,)),
            dma((SUBSTEPS, C, 2)), dma((SUBSTEPS, C, 2)),
            dma((C, Z)), dma((C, Z)),
            dma((C,)), dma((C,)),
            dma((Z,)), dma((1,)),
        ],
        compiler_params=pltpu.CompilerParams(
            collective_id=0, has_side_effects=True, vmem_limit_bytes=48 * 1024 * 1024
        ),
    )(tracers, coef, sunlight, reaction)
    return (east[:, half : half + rows], north[:, half : half + rows], tracers_out, heating)


def solution(mesh):
    C, H, Z = (mesh.shape[a] for a in ("comp", "horiz", "trc"))

    def local(tracers, eastward, *rest):
        dims = (C, H, Z, eastward.shape[0] * C * Z)
        return per_device(dims, tracers, eastward, *rest)

    return jax.shard_map(
        local,
        mesh=mesh,
        in_specs=(
            P(("comp", "trc"), None, "horiz", None),
            P(("comp", "trc"), "horiz", None),
            P(("comp", "trc"), "horiz", None),
            P("horiz", None),
            P("horiz", None),
            P(("comp", "trc"), "horiz", None),
            P("horiz", None),
            P(),
        ),
        out_specs=(
            P(("comp", "trc"), "horiz", None),
            P(("comp", "trc"), "horiz", None),
            P(None, ("comp", "trc"), "horiz", None),
            P(("comp", "trc"), "horiz", None),
        ),
        check_vma=False,
    )
```

```python
import functools

import jax
import jax.numpy as jnp
from jax import lax
from jax.experimental import pallas as pl
from jax.experimental.pallas import tpu as pltpu
from jax.sharding import PartitionSpec as P

SUBSTEPS = 4


TIME_STEP = 0.25
GRAVITY = 1.0
VISCOSITY = 0.05
COURANT = 0.2
HALF_LIGHT = 0.3


TILE = 8
MESH = pl.DeviceIdType.MESH


def remote(src, dst, send, recv, device):
    return pltpu.make_async_remote_copy(
        src_ref=src, dst_ref=dst, send_sem=send, recv_sem=recv, device_id=device, device_id_type=MESH
    )


def kernel(
    dims, east, north, mix, height, mask, tr, sun, react,
    east_out, north_out, out, heat,
    R, T, side, F, CF, W, tot, totr, pre, abv,
    rs, rr, ts, tl, trs, cs, cr, ks, kr, hs, hr, zs, zr, us, ur, bs, br,
):
    C, H, Z, levels = dims
    c, h, z = (lax.axis_index(a) for a in ("comp", "horiz", "trc"))
    group = east.shape[0]
    deep = group * Z
    rows, wide = tr.shape[2], T.shape[3]
    cols = tr.shape[3]
    has_left, has_right = h > 0, h < H - 1

    R[pl.ds(0, group), pl.ds(0, rows)] = east[...]
    R[pl.ds(group, group), pl.ds(0, rows)] = north[...]
    R[pl.ds(2 * group, group), pl.ds(0, rows)] = mix[...]
    R[3 * group, pl.ds(0, rows)] = height[...]
    R[3 * group + 1, pl.ds(0, rows)] = mask[...].astype(jnp.float32)

    @pl.when(h == 0)
    def _():
        R[:, pl.ds(rows + TILE, TILE)] = jnp.zeros((R.shape[0], TILE, cols), jnp.float32)

    @pl.when(h == H - 1)
    def _():
        R[:, pl.ds(rows, TILE)] = jnp.zeros((R.shape[0], TILE, cols), jnp.float32)

    def greet(device):
        pl.semaphore_signal(pltpu.get_barrier_semaphore(), inc=1, device_id=device, device_id_type=MESH)

    for d in range(C):
        c2 = lax.rem(c + d, C)
        if d:
            greet((c2, h, z))
        pl.when(has_left)(functools.partial(greet, (c2, h - 1, z)))
        pl.when(has_right)(functools.partial(greet, (c2, h + 1, z)))
    for d in range(1, Z):
        greet((c, h, lax.rem(z + d, Z)))
    near = has_left.astype(jnp.int32) + has_right.astype(jnp.int32)
    pl.semaphore_wait(pltpu.get_barrier_semaphore(), C * (1 + near) - 1 + Z - 1)

    def coef_copy(up, block):
        where = pl.ds(1 + block * group, group)
        src = CF.at[:, where]
        return remote(src, CF.at[:, where], cs.at[up, block], cr.at[block], (c, h, z + 1 if up else z - 1))

    def tracer_copies(target, source, partner):
        low, high = int(target > 0), int(target < C - 1)
        count = deep + low + high
        src = pl.ds(target * deep - low, count)
        dst = pl.ds(1 - low, count)
        middle = (tr.at[0, src], T.at[0, source, dst, pl.ds(0, rows)])
        left = remote(
            tr.at[0, src, pl.ds(rows - TILE, TILE)], side.at[0, source, dst],
            ts.at[target, 1], trs.at[source, 1], (partner, h + 1, z))
        right = remote(
            tr.at[0, src, pl.ds(0, TILE)], side.at[1, source, dst],
            ts.at[target, 2], trs.at[source, 2], (partner, h - 1, z))
        here = pltpu.make_async_copy(*middle, tl.at[0])
        there = remote(*middle, ts.at[target, 0], trs.at[source, 0], (partner, h, z))
        return here, there, left, right

    to_left = remote(
        R.at[:, pl.ds(0, TILE)], R.at[:, pl.ds(rows, TILE)], rs.at[0], rr.at[0], (c, h - 1, z))
    to_right = remote(
        R.at[:, pl.ds(rows - TILE, TILE)], R.at[:, pl.ds(rows + TILE, TILE)], rs.at[1], rr.at[1], (c, h + 1, z))
    pl.when(has_left)(to_left.start)
    pl.when(has_right)(to_right.start)

    for c2 in range(C):
        here, there, left, right = tracer_copies(c2, c, c2)
        pl.when(c == c2)(here.start)
        pl.when(c != c2)(there.start)
        pl.when(has_right)(left.start)
        pl.when(has_left)(right.start)

    pl.when(has_right)(to_left.wait_recv)
    pl.when(has_left)(to_right.wait_recv)
    ring = rows + 2 * TILE
    lane = lax.broadcasted_iota(jnp.int32, (ring, cols), 1)
    coriolis = 0.5 + 0.5 * lane.astype(jnp.float32) / cols
    sub = lax.broadcasted_iota(jnp.int32, (TILE, cols), 0)

    def next_x(a):
        return pltpu.roll(a, ring - 1, 0)

    def last_x(a):
        return pltpu.roll(a, 1, 0)

    def next_y(a):
        return jnp.where(lane < cols - 1, pltpu.roll(a, cols - 1, 1), 0.0)

    def last_y(a):
        return jnp.where(lane > 0, pltpu.roll(a, 1, 1), 0.0)

    def pack(which, at, a):
        CF[which, at, pl.ds(0, rows)] = a[:rows]
        CF[which, at, pl.ds(rows, TILE)] = jnp.where(
            sub < TILE // 2, a[rows : rows + TILE], a[rows + TILE :])

    @pl.loop(0, group)
    def _(l):
        u, v, eta, wet = R[l], R[group + l], R[3 * group], R[3 * group + 1]
        u_next, v_last = next_y(u), last_y(v)
        u_lap = next_x(u) + last_x(u) + u_next + last_y(u) - 4.0 * u
        v_lap = next_x(v) + last_x(v) + next_y(v) + v_last - 4.0 * v
        v_pair, u_pair = v + v_last, u + u_next
        v_avg = 0.25 * (v_pair + next_x(v_pair))
        u_avg = 0.25 * (u_pair + last_x(u_pair))
        new_u = wet * next_x(wet) * (
            u + TIME_STEP * (coriolis * v_avg - GRAVITY * (next_x(eta) - eta) + VISCOSITY * u_lap))
        new_v = wet * next_y(wet) * (
            v + TIME_STEP * (-coriolis * u_avg - GRAVITY * (next_y(eta) - eta) + VISCOSITY * v_lap))
        speed = jnp.minimum(new_u * new_u + new_v * new_v, 1.0)
        level = z * group + l
        keep = jnp.where(c * deep + level < levels - 1, 1.0, 0.0)
        pack(0, 1 + level, COURANT * new_u)
        pack(1, 1 + level, COURANT * new_v)
        pack(2, 1 + level, wet * R[2 * group + l] * (1.0 + speed) * keep)
        east_out[l] = new_u[:rows]
        north_out[l] = new_v[:rows]

    pl.when(z < Z - 1)(lambda: coef_copy(1, z).start())
    pl.when(z > 0)(lambda: coef_copy(0, z).start())

    @pl.when(h == 0)
    def _():
        side[0] = jnp.zeros(side.shape[1:], jnp.float32)

    @pl.when(h == H - 1)
    def _():
        side[1] = jnp.zeros(side.shape[1:], jnp.float32)

    @pl.when(c == 0)
    def _():
        CF[2, 0] = jnp.zeros((wide, cols), jnp.float32)
        for s in range(SUBSTEPS):
            for k in range(C):
                T[s, k, 0] = jnp.zeros((wide, cols), jnp.float32)
        for k in range(C):
            side[0, k, 0] = jnp.zeros((TILE, cols), jnp.float32)
            side[1, k, 0] = jnp.zeros((TILE, cols), jnp.float32)

    @pl.when(c == C - 1)
    def _():
        for s in range(SUBSTEPS):
            for k in range(C):
                T[s, k, deep + 1] = jnp.zeros((wide, cols), jnp.float32)
        for k in range(C):
            side[0, k, deep + 1] = jnp.zeros((TILE, cols), jnp.float32)
            side[1, k, deep + 1] = jnp.zeros((TILE, cols), jnp.float32)

    def weigh(block):
        @pl.loop(0, group)
        def _(i):
            l = block * group + i
            fx, fy = CF[0, l + 1], CF[1, l + 1]
            px, mx = jnp.maximum(fx, 0.0), jnp.minimum(fx, 0.0)
            py, my = jnp.maximum(fy, 0.0), jnp.minimum(fy, 0.0)
            W[0, l] = 1.0 + pltpu.roll(mx, 1, 0) - px + pltpu.roll(my, 1, 1) - py
            W[1, l] = pltpu.roll(px, 1, 0)
            W[2, l] = -mx
            W[3, l] = pltpu.roll(py, 1, 1)
            W[4, l] = -my

    weigh(z)
    for d in range(1, Z):
        @pl.when(z >= d)
        def _():
            coef_copy(1, z - d).wait_recv()
            pl.when(z < Z - 1)(lambda: coef_copy(1, z - d).start())
            weigh(z - d)

        @pl.when(z + d < Z)
        def _():
            coef_copy(0, z + d).wait_recv()
            pl.when(z > 0)(lambda: coef_copy(0, z + d).start())
            weigh(z + d)

    kup = remote(CF.at[2, deep], CF.at[2, 0], ks.at[0], kr.at[0], (c + 1, h, z))
    pl.when(c < C - 1)(kup.start)
    pl.when(c > 0)(kup.wait_recv)

    def halo(s, k):
        down = remote(T.at[s, k, deep], T.at[s, k, 0], hs.at[s, k, 0], hr.at[s, k, 0], (c + 1, h, z))
        up = remote(T.at[s, k, 1], T.at[s, k, deep + 1], hs.at[s, k, 1], hr.at[s, k, 1], (c - 1, h, z))
        return down, up

    def deliver(k, target, source):
        return remote(
            T.at[SUBSTEPS, k, pl.ds(1 + target * group, group), pl.ds(0, rows)], F.at[k * Z + source],
            zs.at[k, target], zr.at[k, source], (c, h, target))

    def total_copy(target, source):
        return remote(tot, totr.at[source], us.at[target], ur.at[source], (target, h, z))

    def above_copy(target):
        return remote(pre.at[target], abv, bs.at[target], br.at[0], (c, h, target))

    def arrive(k):
        for cc in range(C):
            @pl.when(c == cc)
            def _():
                here, there, left, right = tracer_copies(cc, k, cc)
                pl.when(k == cc)(here.wait)
                pl.when(k != cc)(there.wait_recv)
                pl.when(has_left)(left.wait_recv)
                pl.when(has_right)(right.wait_recv)

        @pl.loop(0, deep + 2)
        def _(l):
            T[0, k, l, pl.ds(rows, TILE)] = jnp.where(sub < TILE // 2, side[1, k, l], side[0, k, l])

    def optics(m):
        return (0.5 + m * m) / levels

    def light_totals():
        run = jnp.zeros((rows, cols), jnp.float32)
        for block in range(Z):
            pre[block] = run
            for l in range(group):
                run = run + optics(T[SUBSTEPS, 0, 1 + block * group + l, pl.ds(0, rows)])
        tot[...] = run
        for c2 in range(1, C):
            pl.when(c < c2)(total_copy(c2, c).start)

    def light_above():
        base = jnp.zeros((rows, cols), jnp.float32)
        abv[...] = base
        for c2 in range(C - 1):
            @pl.when(c > c2)
            def _():
                total_copy(c, c2).wait_recv()
                abv[...] += totr[c2]
        for block in range(1, Z):
            pre[block] = pre[block] + abv[...]
            above_copy(block).start()

    def work(index, carry):
        s, k = index // C, lax.rem(index, C)
        pl.when(s == 0)(functools.partial(arrive, k))

        @pl.when(s > 0)
        def _():
            down, up = halo(s, k)
            pl.when(c > 0)(down.wait_recv)
            pl.when(c < C - 1)(up.wait_recv)

        pl.when((s == SUBSTEPS - 1) & (k == C - 1) & (z == 0))(light_above)

        def level(l, carry):
            up, mid, down = T[s, k, l], T[s, k, l + 1], T[s, k, l + 2]
            T[s + 1, k, l + 1] = (
                W[0, l] * mid + W[1, l] * pltpu.roll(mid, 1, 0) + W[2, l] * pltpu.roll(mid, wide - 1, 0)
                + W[3, l] * pltpu.roll(mid, 1, 1) + W[4, l] * pltpu.roll(mid, cols - 1, 1)
                + CF[2, l + 1] * (down - mid) + CF[2, l] * (up - mid)
            )
            return carry

        lax.fori_loop(0, deep, level, 0, unroll=2)

        @pl.when(s < SUBSTEPS - 1)
        def _():
            down, up = halo(s + 1, k)
            pl.when(c < C - 1)(down.start)
            pl.when(c > 0)(up.start)

        @pl.when(s == SUBSTEPS - 1)
        def _():
            for d in range(1, Z):
                deliver(k, lax.rem(z + d, Z), z).start()
            F[k * Z + z] = T[SUBSTEPS, k, pl.ds(1 + z * group, group), pl.ds(0, rows)]
            pl.when((k == 0) & (z == 0))(light_totals)

        return carry

    lax.fori_loop(0, SUBSTEPS * C, work, 0)

    pl.when(z > 0)(above_copy(z).wait_recv)
    for k in range(C):
        for d in range(1, Z):
            deliver(k, z, lax.rem(z + d, Z)).wait_recv()

    def react_tile(index, carry):
        l, r = index // (rows // TILE), lax.rem(index, rows // TILE)
        here = pl.ds(pl.multiple_of(r * TILE, TILE), TILE)
        field = [F[j, l, here] for j in range(F.shape[0])]
        tau = optics(field[0])
        depth = abv[here]
        abv[here] = depth + tau
        light_top = sun[here] * jnp.exp(-depth)
        heat[l, here] = levels * light_top * (1.0 - jnp.exp(-tau))
        light_mid = light_top * jnp.exp(-0.5 * tau)
        limit = light_mid / (light_mid + HALF_LIGHT)
        for i in range(F.shape[0]):
            growth = react[i, 0] * field[0]
            for j in range(1, F.shape[0]):
                growth = growth + react[i, j] * field[j]
            out[i, l, here] = field[i] + limit * growth
        return carry

    lax.fori_loop(0, group * (rows // TILE), react_tile, 0)

    pl.when(has_left)(to_left.wait_send)
    pl.when(has_right)(to_right.wait_send)
    pl.when(z < Z - 1)(lambda: coef_copy(1, z).wait_send())
    pl.when(z > 0)(lambda: coef_copy(0, z).wait_send())
    for d in range(1, Z):
        pl.when((z >= d) & (z < Z - 1))(lambda: coef_copy(1, z - d).wait_send())
        pl.when((z + d < Z) & (z > 0))(lambda: coef_copy(0, z + d).wait_send())
    for c2 in range(C):
        here, there, left, right = tracer_copies(c2, c, c2)
        pl.when(c != c2)(there.wait_send)
        pl.when(has_right)(left.wait_send)
        pl.when(has_left)(right.wait_send)
    pl.when(c < C - 1)(kup.wait_send)
    for s in range(1, SUBSTEPS):
        for k in range(C):
            down, up = halo(s, k)
            pl.when(c < C - 1)(down.wait_send)
            pl.when(c > 0)(up.wait_send)
    for k in range(C):
        for d in range(1, Z):
            deliver(k, lax.rem(z + d, Z), z).wait_send()

    @pl.when(z == 0)
    def _():
        for c2 in range(1, C):
            pl.when(c < c2)(total_copy(c2, c).wait_send)
        for block in range(1, Z):
            above_copy(block).wait_send()


def per_device(dims, tracers, eastward, northward, surface_height, sea_mask, mixing, sunlight, reaction):
    C, H, Z, levels = dims
    group, rows, cols = eastward.shape
    wide, deep, f32 = rows + TILE, group * Z, jnp.float32
    dma = pltpu.SemaphoreType.DMA
    vmem = pl.BlockSpec(memory_space=pltpu.VMEM)
    plane = jax.ShapeDtypeStruct((group, rows, cols), f32)
    return pl.pallas_call(
        functools.partial(kernel, dims),
        out_shape=(
            plane, plane, jax.ShapeDtypeStruct((C * Z, group, rows, cols), f32), plane,
        ),
        in_specs=[vmem] * 5 + [pl.BlockSpec(memory_space=pl.ANY), vmem, pl.BlockSpec(memory_space=pltpu.SMEM)],
        out_specs=(vmem,) * 4,
        scratch_shapes=[
            pltpu.VMEM((3 * group + 2, rows + 2 * TILE, cols), f32),
            pltpu.VMEM((SUBSTEPS + 1, C, deep + 2, wide, cols), f32),
            pltpu.VMEM((2, C, deep + 2, TILE, cols), f32),
            pltpu.VMEM((C * Z, group, rows, cols), f32),
            pltpu.VMEM((3, deep + 1, wide, cols), f32),
            pltpu.VMEM((5, deep, wide, cols), f32),
            pltpu.VMEM((rows, cols), f32),
            pltpu.VMEM((C, rows, cols), f32),
            pltpu.VMEM((Z, rows, cols), f32),
            pltpu.VMEM((rows, cols), f32),
            dma((2,)), dma((2,)),
            dma((C, 3)), dma((1,)), dma((C, 3)),
            dma((2, Z)), dma((Z,)),
            dma((1,)), dma((1,)),
            dma((SUBSTEPS, C, 2)), dma((SUBSTEPS, C, 2)),
            dma((C, Z)), dma((C, Z)),
            dma((C,)), dma((C,)),
            dma((Z,)), dma((1,)),
        ],
        compiler_params=pltpu.CompilerParams(
            collective_id=0, has_side_effects=True, vmem_limit_bytes=48 * 1024 * 1024
        ),
    )(eastward, northward, mixing, surface_height, sea_mask, tracers, sunlight, reaction)


def solution(mesh):
    C, H, Z = (mesh.shape[a] for a in ("comp", "horiz", "trc"))

    def local(tracers, eastward, *rest):
        dims = (C, H, Z, eastward.shape[0] * C * Z)
        return per_device(dims, tracers, eastward, *rest)

    return jax.shard_map(
        local,
        mesh=mesh,
        in_specs=(
            P(("comp", "trc"), None, "horiz", None),
            P(("comp", "trc"), "horiz", None),
            P(("comp", "trc"), "horiz", None),
            P("horiz", None),
            P("horiz", None),
            P(("comp", "trc"), "horiz", None),
            P("horiz", None),
            P(),
        ),
        out_specs=(
            P(("comp", "trc"), "horiz", None),
            P(("comp", "trc"), "horiz", None),
            P(None, ("comp", "trc"), "horiz", None),
            P(("comp", "trc"), "horiz", None),
        ),
        check_vma=False,
    )
```

```python
import functools

import jax
import jax.numpy as jnp
from jax import lax
from jax.experimental import pallas as pl
from jax.experimental.pallas import tpu as pltpu
from jax.sharding import PartitionSpec as P

SUBSTEPS = 4


TIME_STEP = 0.25
GRAVITY = 1.0
VISCOSITY = 0.05
COURANT = 0.2
HALF_LIGHT = 0.3


TILE = 8
MESH = pl.DeviceIdType.MESH


def remote(src, dst, send, recv, device):
    return pltpu.make_async_remote_copy(
        src_ref=src, dst_ref=dst, send_sem=send, recv_sem=recv, device_id=device, device_id_type=MESH
    )


def kernel(
    dims, east, north, mix, height, mask, tr, sunlight, react,
    east_out, north_out, out, heat,
    R, sea, sun, T, side, F, CF, W, tot, totr, pre, abv,
    ls, rs, rr, ts, tl, trs, cs, cr, ks, kr, hs, hr, zs, zr, us, ur, bs, br,
):
    C, H, Z, levels = dims
    c, h, z = (lax.axis_index(a) for a in ("comp", "horiz", "trc"))
    group = east.shape[0]
    deep = group * Z
    rows, wide = tr.shape[2], T.shape[3]
    cols = tr.shape[3]
    has_left, has_right = h > 0, h < H - 1

    loads = [
        pltpu.make_async_copy(src, dst, ls.at[i])
        for i, (src, dst) in enumerate((
            (east, R.at[pl.ds(0, group), pl.ds(0, rows)]),
            (north, R.at[pl.ds(group, group), pl.ds(0, rows)]),
            (mix, R.at[pl.ds(2 * group, group), pl.ds(0, rows)]),
            (height, R.at[3 * group, pl.ds(0, rows)]),
            (mask, sea),
            (sunlight, sun),
        ))
    ]
    for load in loads:
        load.start()

    @pl.when(h == 0)
    def _():
        R[:, pl.ds(rows + TILE, TILE)] = jnp.zeros((R.shape[0], TILE, cols), jnp.float32)

    @pl.when(h == H - 1)
    def _():
        R[:, pl.ds(rows, TILE)] = jnp.zeros((R.shape[0], TILE, cols), jnp.float32)

    def greet(device):
        pl.semaphore_signal(pltpu.get_barrier_semaphore(), inc=1, device_id=device, device_id_type=MESH)

    for d in range(C):
        c2 = lax.rem(c + d, C)
        if d:
            greet((c2, h, z))
        pl.when(has_left)(functools.partial(greet, (c2, h - 1, z)))
        pl.when(has_right)(functools.partial(greet, (c2, h + 1, z)))
    for d in range(1, Z):
        greet((c, h, lax.rem(z + d, Z)))
    near = has_left.astype(jnp.int32) + has_right.astype(jnp.int32)
    pl.semaphore_wait(pltpu.get_barrier_semaphore(), C * (1 + near) - 1 + Z - 1)

    def coef_copy(up, block):
        where = pl.ds(1 + block * group, group)
        src = CF.at[:, where]
        return remote(src, CF.at[:, where], cs.at[up, block], cr.at[block], (c, h, z + 1 if up else z - 1))

    def tracer_copies(target, source, partner):
        low, high = int(target > 0), int(target < C - 1)
        count = deep + low + high
        src = pl.ds(target * deep - low, count)
        dst = pl.ds(1 - low, count)
        middle = (tr.at[0, src], T.at[0, source, dst, pl.ds(0, rows)])
        left = remote(
            tr.at[0, src, pl.ds(rows - TILE, TILE)], side.at[0, source, dst],
            ts.at[target, 1], trs.at[source, 1], (partner, h + 1, z))
        right = remote(
            tr.at[0, src, pl.ds(0, TILE)], side.at[1, source, dst],
            ts.at[target, 2], trs.at[source, 2], (partner, h - 1, z))
        here = pltpu.make_async_copy(*middle, tl.at[0])
        there = remote(*middle, ts.at[target, 0], trs.at[source, 0], (partner, h, z))
        return here, there, left, right

    for load in loads:
        load.wait()
    R[3 * group + 1, pl.ds(0, rows)] = sea[...].astype(jnp.float32)

    to_left = remote(
        R.at[:, pl.ds(0, TILE)], R.at[:, pl.ds(rows, TILE)], rs.at[0], rr.at[0], (c, h - 1, z))
    to_right = remote(
        R.at[:, pl.ds(rows - TILE, TILE)], R.at[:, pl.ds(rows + TILE, TILE)], rs.at[1], rr.at[1], (c, h + 1, z))
    pl.when(has_left)(to_left.start)
    pl.when(has_right)(to_right.start)

    for c2 in range(C):
        here, there, left, right = tracer_copies(c2, c, c2)
        pl.when(c == c2)(here.start)
        pl.when(c != c2)(there.start)
        pl.when(has_right)(left.start)
        pl.when(has_left)(right.start)

    pl.when(has_right)(to_left.wait_recv)
    pl.when(has_left)(to_right.wait_recv)
    ring = rows + 2 * TILE
    lane = lax.broadcasted_iota(jnp.int32, (ring, cols), 1)
    coriolis = 0.5 + 0.5 * lane.astype(jnp.float32) / cols
    sub = lax.broadcasted_iota(jnp.int32, (TILE, cols), 0)

    def next_x(a):
        return pltpu.roll(a, ring - 1, 0)

    def last_x(a):
        return pltpu.roll(a, 1, 0)

    def next_y(a):
        return jnp.where(lane < cols - 1, pltpu.roll(a, cols - 1, 1), 0.0)

    def last_y(a):
        return jnp.where(lane > 0, pltpu.roll(a, 1, 1), 0.0)

    def pack(which, at, a):
        CF[which, at, pl.ds(0, rows)] = a[:rows]
        CF[which, at, pl.ds(rows, TILE)] = jnp.where(
            sub < TILE // 2, a[rows : rows + TILE], a[rows + TILE :])

    @pl.loop(0, group)
    def _(l):
        u, v, eta, wet = R[l], R[group + l], R[3 * group], R[3 * group + 1]
        u_next, v_last = next_y(u), last_y(v)
        u_lap = next_x(u) + last_x(u) + u_next + last_y(u) - 4.0 * u
        v_lap = next_x(v) + last_x(v) + next_y(v) + v_last - 4.0 * v
        v_pair, u_pair = v + v_last, u + u_next
        v_avg = 0.25 * (v_pair + next_x(v_pair))
        u_avg = 0.25 * (u_pair + last_x(u_pair))
        new_u = wet * next_x(wet) * (
            u + TIME_STEP * (coriolis * v_avg - GRAVITY * (next_x(eta) - eta) + VISCOSITY * u_lap))
        new_v = wet * next_y(wet) * (
            v + TIME_STEP * (-coriolis * u_avg - GRAVITY * (next_y(eta) - eta) + VISCOSITY * v_lap))
        speed = jnp.minimum(new_u * new_u + new_v * new_v, 1.0)
        level = z * group + l
        keep = jnp.where(c * deep + level < levels - 1, 1.0, 0.0)
        pack(0, 1 + level, COURANT * new_u)
        pack(1, 1 + level, COURANT * new_v)
        pack(2, 1 + level, wet * R[2 * group + l] * (1.0 + speed) * keep)
        east_out[l] = new_u[:rows]
        north_out[l] = new_v[:rows]

    pl.when(z < Z - 1)(lambda: coef_copy(1, z).start())
    pl.when(z > 0)(lambda: coef_copy(0, z).start())

    @pl.when(h == 0)
    def _():
        side[0] = jnp.zeros(side.shape[1:], jnp.float32)

    @pl.when(h == H - 1)
    def _():
        side[1] = jnp.zeros(side.shape[1:], jnp.float32)

    @pl.when(c == 0)
    def _():
        CF[2, 0] = jnp.zeros((wide, cols), jnp.float32)
        for s in range(SUBSTEPS):
            for k in range(C):
                T[s, k, 0] = jnp.zeros((wide, cols), jnp.float32)
        for k in range(C):
            side[0, k, 0] = jnp.zeros((TILE, cols), jnp.float32)
            side[1, k, 0] = jnp.zeros((TILE, cols), jnp.float32)

    @pl.when(c == C - 1)
    def _():
        for s in range(SUBSTEPS):
            for k in range(C):
                T[s, k, deep + 1] = jnp.zeros((wide, cols), jnp.float32)
        for k in range(C):
            side[0, k, deep + 1] = jnp.zeros((TILE, cols), jnp.float32)
            side[1, k, deep + 1] = jnp.zeros((TILE, cols), jnp.float32)

    def weigh(block):
        @pl.loop(0, group)
        def _(i):
            l = block * group + i
            fx, fy = CF[0, l + 1], CF[1, l + 1]
            px, mx = jnp.maximum(fx, 0.0), jnp.minimum(fx, 0.0)
            py, my = jnp.maximum(fy, 0.0), jnp.minimum(fy, 0.0)
            W[0, l] = 1.0 + pltpu.roll(mx, 1, 0) - px + pltpu.roll(my, 1, 1) - py
            W[1, l] = pltpu.roll(px, 1, 0)
            W[2, l] = -mx
            W[3, l] = pltpu.roll(py, 1, 1)
            W[4, l] = -my

    weigh(z)
    for d in range(1, Z):
        @pl.when(z >= d)
        def _():
            coef_copy(1, z - d).wait_recv()
            pl.when(z < Z - 1)(lambda: coef_copy(1, z - d).start())

        @pl.when(z + d < Z)
        def _():
            coef_copy(0, z + d).wait_recv()
            pl.when(z > 0)(lambda: coef_copy(0, z + d).start())

        pl.when(z >= d)(functools.partial(weigh, z - d))
        pl.when(z + d < Z)(functools.partial(weigh, z + d))

    kup = remote(CF.at[2, deep], CF.at[2, 0], ks.at[0], kr.at[0], (c + 1, h, z))
    pl.when(c < C - 1)(kup.start)
    pl.when(c > 0)(kup.wait_recv)

    def halo(s, k):
        down = remote(T.at[s, k, deep], T.at[s, k, 0], hs.at[s, k, 0], hr.at[s, k, 0], (c + 1, h, z))
        up = remote(T.at[s, k, 1], T.at[s, k, deep + 1], hs.at[s, k, 1], hr.at[s, k, 1], (c - 1, h, z))
        return down, up

    def deliver(k, target, source):
        return remote(
            T.at[SUBSTEPS, k, pl.ds(1 + target * group, group), pl.ds(0, rows)], F.at[k * Z + source],
            zs.at[k, target], zr.at[k, source], (c, h, target))

    def total_copy(target, source):
        return remote(tot, totr.at[source], us.at[target], ur.at[source], (target, h, z))

    def above_copy(target):
        return remote(pre.at[target], abv, bs.at[target], br.at[0], (c, h, target))

    def arrive(k):
        for cc in range(C):
            @pl.when(c == cc)
            def _():
                here, there, left, right = tracer_copies(cc, k, cc)
                pl.when(k == cc)(here.wait)
                pl.when(k != cc)(there.wait_recv)
                pl.when(has_left)(left.wait_recv)
                pl.when(has_right)(right.wait_recv)

        @pl.loop(0, deep + 2)
        def _(l):
            T[0, k, l, pl.ds(rows, TILE)] = jnp.where(sub < TILE // 2, side[1, k, l], side[0, k, l])

    def optics(m):
        return (0.5 + m * m) / levels

    def light_totals():
        run = jnp.zeros((rows, cols), jnp.float32)
        for block in range(Z):
            pre[block] = run
            for l in range(group):
                run = run + optics(T[SUBSTEPS, 0, 1 + block * group + l, pl.ds(0, rows)])
        tot[...] = run
        for c2 in range(1, C):
            pl.when(c < c2)(total_copy(c2, c).start)

    def light_above():
        base = jnp.zeros((rows, cols), jnp.float32)
        abv[...] = base
        for c2 in range(C - 1):
            @pl.when(c > c2)
            def _():
                total_copy(c, c2).wait_recv()
                abv[...] += totr[c2]
        for block in range(1, Z):
            pre[block] = pre[block] + abv[...]
            above_copy(block).start()

    def work(index, carry):
        s, k = index // C, lax.rem(index, C)
        pl.when(s == 0)(functools.partial(arrive, k))

        @pl.when(s > 0)
        def _():
            down, up = halo(s, k)
            pl.when(c > 0)(down.wait_recv)
            pl.when(c < C - 1)(up.wait_recv)

        pl.when((s == SUBSTEPS - 1) & (k == C - 1) & (z == 0))(light_above)

        def level(l, carry):
            up, mid, down = T[s, k, l], T[s, k, l + 1], T[s, k, l + 2]
            T[s + 1, k, l + 1] = (
                W[0, l] * mid + W[1, l] * pltpu.roll(mid, 1, 0) + W[2, l] * pltpu.roll(mid, wide - 1, 0)
                + W[3, l] * pltpu.roll(mid, 1, 1) + W[4, l] * pltpu.roll(mid, cols - 1, 1)
                + CF[2, l + 1] * (down - mid) + CF[2, l] * (up - mid)
            )
            return carry

        lax.fori_loop(0, deep, level, 0, unroll=2)

        @pl.when(s < SUBSTEPS - 1)
        def _():
            down, up = halo(s + 1, k)
            pl.when(c < C - 1)(down.start)
            pl.when(c > 0)(up.start)

        @pl.when(s == SUBSTEPS - 1)
        def _():
            for d in range(1, Z):
                deliver(k, lax.rem(z + d, Z), z).start()
            F[k * Z + z] = T[SUBSTEPS, k, pl.ds(1 + z * group, group), pl.ds(0, rows)]
            pl.when((k == 0) & (z == 0))(light_totals)

        return carry

    lax.fori_loop(0, SUBSTEPS * C, work, 0)

    pl.when(z > 0)(above_copy(z).wait_recv)
    for k in range(C):
        for d in range(1, Z):
            deliver(k, z, lax.rem(z + d, Z)).wait_recv()

    def react_tile(index, carry):
        l, r = index // (rows // TILE), lax.rem(index, rows // TILE)
        here = pl.ds(pl.multiple_of(r * TILE, TILE), TILE)
        field = [F[j, l, here] for j in range(F.shape[0])]
        tau = optics(field[0])
        depth = abv[here]
        abv[here] = depth + tau
        light_top = sun[here] * jnp.exp(-depth)
        heat[l, here] = levels * light_top * (1.0 - jnp.exp(-tau))
        light_mid = light_top * jnp.exp(-0.5 * tau)
        limit = light_mid / (light_mid + HALF_LIGHT)
        for i in range(F.shape[0]):
            growth = react[i, 0] * field[0]
            for j in range(1, F.shape[0]):
                growth = growth + react[i, j] * field[j]
            out[i, l, here] = field[i] + limit * growth
        return carry

    lax.fori_loop(0, group * (rows // TILE), react_tile, 0)

    pl.when(has_left)(to_left.wait_send)
    pl.when(has_right)(to_right.wait_send)
    pl.when(z < Z - 1)(lambda: coef_copy(1, z).wait_send())
    pl.when(z > 0)(lambda: coef_copy(0, z).wait_send())
    for d in range(1, Z):
        pl.when((z >= d) & (z < Z - 1))(lambda: coef_copy(1, z - d).wait_send())
        pl.when((z + d < Z) & (z > 0))(lambda: coef_copy(0, z + d).wait_send())
    for c2 in range(C):
        here, there, left, right = tracer_copies(c2, c, c2)
        pl.when(c != c2)(there.wait_send)
        pl.when(has_right)(left.wait_send)
        pl.when(has_left)(right.wait_send)
    pl.when(c < C - 1)(kup.wait_send)
    for s in range(1, SUBSTEPS):
        for k in range(C):
            down, up = halo(s, k)
            pl.when(c < C - 1)(down.wait_send)
            pl.when(c > 0)(up.wait_send)
    for k in range(C):
        for d in range(1, Z):
            deliver(k, lax.rem(z + d, Z), z).wait_send()

    @pl.when(z == 0)
    def _():
        for c2 in range(1, C):
            pl.when(c < c2)(total_copy(c2, c).wait_send)
        for block in range(1, Z):
            above_copy(block).wait_send()


def per_device(dims, tracers, eastward, northward, surface_height, sea_mask, mixing, sunlight, reaction):
    C, H, Z, levels = dims
    group, rows, cols = eastward.shape
    wide, deep, f32 = rows + TILE, group * Z, jnp.float32
    dma = pltpu.SemaphoreType.DMA
    vmem = pl.BlockSpec(memory_space=pltpu.VMEM)
    plane = jax.ShapeDtypeStruct((group, rows, cols), f32)
    return pl.pallas_call(
        functools.partial(kernel, dims),
        out_shape=(
            plane, plane, jax.ShapeDtypeStruct((C * Z, group, rows, cols), f32), plane,
        ),
        in_specs=[pl.BlockSpec(memory_space=pltpu.HBM)] * 7 + [pl.BlockSpec(memory_space=pltpu.SMEM)],
        out_specs=(vmem,) * 4,
        scratch_shapes=[
            pltpu.VMEM((3 * group + 2, rows + 2 * TILE, cols), f32),
            pltpu.VMEM((rows, cols), jnp.int32), pltpu.VMEM((rows, cols), f32),
            pltpu.VMEM((SUBSTEPS + 1, C, deep + 2, wide, cols), f32),
            pltpu.VMEM((2, C, deep + 2, TILE, cols), f32),
            pltpu.VMEM((C * Z, group, rows, cols), f32),
            pltpu.VMEM((3, deep + 1, wide, cols), f32),
            pltpu.VMEM((5, deep, wide, cols), f32),
            pltpu.VMEM((rows, cols), f32),
            pltpu.VMEM((C, rows, cols), f32),
            pltpu.VMEM((Z, rows, cols), f32),
            pltpu.VMEM((rows, cols), f32),
            dma((6,)), dma((2,)), dma((2,)),
            dma((C, 3)), dma((1,)), dma((C, 3)),
            dma((2, Z)), dma((Z,)),
            dma((1,)), dma((1,)),
            dma((SUBSTEPS, C, 2)), dma((SUBSTEPS, C, 2)),
            dma((C, Z)), dma((C, Z)),
            dma((C,)), dma((C,)),
            dma((Z,)), dma((1,)),
        ],
        compiler_params=pltpu.CompilerParams(
            collective_id=0, has_side_effects=True, vmem_limit_bytes=63 * 1024 * 1024
        ),
    )(eastward, northward, mixing, surface_height, sea_mask, tracers, sunlight, reaction)


def solution(mesh):
    C, H, Z = (mesh.shape[a] for a in ("comp", "horiz", "trc"))

    def local(tracers, eastward, *rest):
        dims = (C, H, Z, eastward.shape[0] * C * Z)
        return per_device(dims, tracers, eastward, *rest)

    return jax.shard_map(
        local,
        mesh=mesh,
        in_specs=(
            P(("comp", "trc"), None, "horiz", None),
            P(("comp", "trc"), "horiz", None),
            P(("comp", "trc"), "horiz", None),
            P("horiz", None),
            P("horiz", None),
            P(("comp", "trc"), "horiz", None),
            P("horiz", None),
            P(),
        ),
        out_specs=(
            P(("comp", "trc"), "horiz", None),
            P(("comp", "trc"), "horiz", None),
            P(None, ("comp", "trc"), "horiz", None),
            P(("comp", "trc"), "horiz", None),
        ),
        check_vma=False,
    )
```

```python
import functools

import jax
import jax.numpy as jnp
from jax import lax
from jax.experimental import pallas as pl
from jax.experimental.pallas import tpu as pltpu
from jax.sharding import PartitionSpec as P

SUBSTEPS = 4


TIME_STEP = 0.25
GRAVITY = 1.0
VISCOSITY = 0.05
COURANT = 0.2
HALF_LIGHT = 0.3


TILE = 8
MESH = pl.DeviceIdType.MESH


def remote(src, dst, send, recv, device):
    return pltpu.make_async_remote_copy(
        src_ref=src, dst_ref=dst, send_sem=send, recv_sem=recv, device_id=device, device_id_type=MESH
    )


def kernel(
    dims, east, north, mix, height, mask, tr, sunlight, react,
    east_out, north_out, out, heat,
    R, sea, sun, T, side, F, CF, W, tot, totr, pre, abv,
    ls, rs, rr, ts, tl, trs, cs, cr, ks, kr, hs, hr, zs, zr, us, ur, bs, br,
):
    C, H, Z, levels = dims
    c, h, z = (lax.axis_index(a) for a in ("comp", "horiz", "trc"))
    group = east.shape[0]
    deep = group * Z
    rows, wide = tr.shape[2], T.shape[3]
    cols = tr.shape[3]
    has_left, has_right = h > 0, h < H - 1

    loads = [
        pltpu.make_async_copy(src, dst, ls.at[i])
        for i, (src, dst) in enumerate((
            (east, R.at[pl.ds(0, group), pl.ds(0, rows)]),
            (north, R.at[pl.ds(group, group), pl.ds(0, rows)]),
            (mix, R.at[pl.ds(2 * group, group), pl.ds(0, rows)]),
            (height, R.at[3 * group, pl.ds(0, rows)]),
            (mask, sea),
            (sunlight, sun),
        ))
    ]
    for load in loads:
        load.start()

    @pl.when(h == 0)
    def _():
        R[:, pl.ds(rows + TILE, TILE)] = jnp.zeros((R.shape[0], TILE, cols), jnp.float32)

    @pl.when(h == H - 1)
    def _():
        R[:, pl.ds(rows, TILE)] = jnp.zeros((R.shape[0], TILE, cols), jnp.float32)

    def greet(device):
        pl.semaphore_signal(pltpu.get_barrier_semaphore(), inc=1, device_id=device, device_id_type=MESH)

    for d in range(C):
        c2 = lax.rem(c + d, C)
        if d:
            greet((c2, h, z))
        pl.when(has_left)(functools.partial(greet, (c2, h - 1, z)))
        pl.when(has_right)(functools.partial(greet, (c2, h + 1, z)))
    for d in range(1, Z):
        greet((c, h, lax.rem(z + d, Z)))
    near = has_left.astype(jnp.int32) + has_right.astype(jnp.int32)
    pl.semaphore_wait(pltpu.get_barrier_semaphore(), C * (1 + near) - 1 + Z - 1)

    def coef_copy(up, block):
        where = pl.ds(1 + block * group, group)
        src = CF.at[:, where]
        return remote(src, CF.at[:, where], cs.at[up, block], cr.at[block], (c, h, z + 1 if up else z - 1))

    def tracer_copies(target, source, partner):
        low, high = int(target > 0), int(target < C - 1)
        count = deep + low + high
        src = pl.ds(target * deep - low, count)
        dst = pl.ds(1 - low, count)
        middle = (tr.at[0, src], T.at[0, source, dst, pl.ds(0, rows)])
        left = remote(
            tr.at[0, src, pl.ds(rows - TILE, TILE)], side.at[0, source, dst],
            ts.at[target, 1], trs.at[source, 1], (partner, h + 1, z))
        right = remote(
            tr.at[0, src, pl.ds(0, TILE)], side.at[1, source, dst],
            ts.at[target, 2], trs.at[source, 2], (partner, h - 1, z))
        here = pltpu.make_async_copy(*middle, tl.at[0])
        there = remote(*middle, ts.at[target, 0], trs.at[source, 0], (partner, h, z))
        return here, there, left, right

    for load in loads:
        load.wait()
    R[3 * group + 1, pl.ds(0, rows)] = sea[...].astype(jnp.float32)

    to_left = remote(
        R.at[:, pl.ds(0, TILE)], R.at[:, pl.ds(rows, TILE)], rs.at[0], rr.at[0], (c, h - 1, z))
    to_right = remote(
        R.at[:, pl.ds(rows - TILE, TILE)], R.at[:, pl.ds(rows + TILE, TILE)], rs.at[1], rr.at[1], (c, h + 1, z))
    pl.when(has_left)(to_left.start)
    pl.when(has_right)(to_right.start)

    def send_tracer(stage):
        for cc in range(C):
            half = max(C // 2, 1)
            order = sorted(range(C), key=lambda t: (t // half == cc // half, (t - cc) % C))
            order = [t for t in order if t != cc] + [cc]
            target = order[stage]

            @pl.when(c == cc)
            def _():
                here, there, left, right = tracer_copies(target, cc, target)
                (here if target == cc else there).start()
                pl.when(has_right)(left.start)
                pl.when(has_left)(right.start)

    send_tracer(0)

    pl.when(has_right)(to_left.wait_recv)
    pl.when(has_left)(to_right.wait_recv)
    ring = rows + 2 * TILE
    lane = lax.broadcasted_iota(jnp.int32, (ring, cols), 1)
    coriolis = 0.5 + 0.5 * lane.astype(jnp.float32) / cols
    sub = lax.broadcasted_iota(jnp.int32, (TILE, cols), 0)

    def next_x(a):
        return pltpu.roll(a, ring - 1, 0)

    def last_x(a):
        return pltpu.roll(a, 1, 0)

    def next_y(a):
        return jnp.where(lane < cols - 1, pltpu.roll(a, cols - 1, 1), 0.0)

    def last_y(a):
        return jnp.where(lane > 0, pltpu.roll(a, 1, 1), 0.0)

    def pack(which, at, a):
        CF[which, at, pl.ds(0, rows)] = a[:rows]
        CF[which, at, pl.ds(rows, TILE)] = jnp.where(
            sub < TILE // 2, a[rows : rows + TILE], a[rows + TILE :])

    @pl.loop(0, group)
    def _(l):
        u, v, eta, wet = R[l], R[group + l], R[3 * group], R[3 * group + 1]
        u_next, v_last = next_y(u), last_y(v)
        u_lap = next_x(u) + last_x(u) + u_next + last_y(u) - 4.0 * u
        v_lap = next_x(v) + last_x(v) + next_y(v) + v_last - 4.0 * v
        v_pair, u_pair = v + v_last, u + u_next
        v_avg = 0.25 * (v_pair + next_x(v_pair))
        u_avg = 0.25 * (u_pair + last_x(u_pair))
        new_u = wet * next_x(wet) * (
            u + TIME_STEP * (coriolis * v_avg - GRAVITY * (next_x(eta) - eta) + VISCOSITY * u_lap))
        new_v = wet * next_y(wet) * (
            v + TIME_STEP * (-coriolis * u_avg - GRAVITY * (next_y(eta) - eta) + VISCOSITY * v_lap))
        speed = jnp.minimum(new_u * new_u + new_v * new_v, 1.0)
        level = z * group + l
        keep = jnp.where(c * deep + level < levels - 1, 1.0, 0.0)
        pack(0, 1 + level, COURANT * new_u)
        pack(1, 1 + level, COURANT * new_v)
        pack(2, 1 + level, wet * R[2 * group + l] * (1.0 + speed) * keep)
        east_out[l] = new_u[:rows]
        north_out[l] = new_v[:rows]

    pl.when(z < Z - 1)(lambda: coef_copy(1, z).start())
    pl.when(z > 0)(lambda: coef_copy(0, z).start())

    @pl.when(h == 0)
    def _():
        side[0] = jnp.zeros(side.shape[1:], jnp.float32)

    @pl.when(h == H - 1)
    def _():
        side[1] = jnp.zeros(side.shape[1:], jnp.float32)

    @pl.when(c == 0)
    def _():
        CF[2, 0] = jnp.zeros((wide, cols), jnp.float32)
        for s in range(SUBSTEPS):
            for k in range(C):
                T[s, k, 0] = jnp.zeros((wide, cols), jnp.float32)
        for k in range(C):
            side[0, k, 0] = jnp.zeros((TILE, cols), jnp.float32)
            side[1, k, 0] = jnp.zeros((TILE, cols), jnp.float32)

    @pl.when(c == C - 1)
    def _():
        for s in range(SUBSTEPS):
            for k in range(C):
                T[s, k, deep + 1] = jnp.zeros((wide, cols), jnp.float32)
        for k in range(C):
            side[0, k, deep + 1] = jnp.zeros((TILE, cols), jnp.float32)
            side[1, k, deep + 1] = jnp.zeros((TILE, cols), jnp.float32)

    def weigh(block):
        @pl.loop(0, group)
        def _(i):
            l = block * group + i
            fx, fy = CF[0, l + 1], CF[1, l + 1]
            px, mx = jnp.maximum(fx, 0.0), jnp.minimum(fx, 0.0)
            py, my = jnp.maximum(fy, 0.0), jnp.minimum(fy, 0.0)
            W[0, l] = 1.0 + pltpu.roll(mx, 1, 0) - px + pltpu.roll(my, 1, 1) - py
            W[1, l] = pltpu.roll(px, 1, 0)
            W[2, l] = -mx
            W[3, l] = pltpu.roll(py, 1, 1)
            W[4, l] = -my

    if C > 1:
        send_tracer(1)
    weigh(z)
    for d in range(1, Z):
        @pl.when(z >= d)
        def _():
            coef_copy(1, z - d).wait_recv()
            pl.when(z < Z - 1)(lambda: coef_copy(1, z - d).start())

        @pl.when(z + d < Z)
        def _():
            coef_copy(0, z + d).wait_recv()
            pl.when(z > 0)(lambda: coef_copy(0, z + d).start())

        if d + 1 < C:
            send_tracer(d + 1)
        pl.when(z >= d)(functools.partial(weigh, z - d))
        pl.when(z + d < Z)(functools.partial(weigh, z + d))

    for stage in range(max(Z, 2), C):
        send_tracer(stage)

    kup = remote(CF.at[2, deep], CF.at[2, 0], ks.at[0], kr.at[0], (c + 1, h, z))
    pl.when(c < C - 1)(kup.start)
    pl.when(c > 0)(kup.wait_recv)

    def halo(s, k):
        down = remote(T.at[s, k, deep], T.at[s, k, 0], hs.at[s, k, 0], hr.at[s, k, 0], (c + 1, h, z))
        up = remote(T.at[s, k, 1], T.at[s, k, deep + 1], hs.at[s, k, 1], hr.at[s, k, 1], (c - 1, h, z))
        return down, up

    def deliver(k, target, source):
        return remote(
            T.at[SUBSTEPS, k, pl.ds(1 + target * group, group), pl.ds(0, rows)], F.at[k * Z + source],
            zs.at[k, target], zr.at[k, source], (c, h, target))

    def total_copy(target, source):
        return remote(tot, totr.at[source], us.at[target], ur.at[source], (target, h, z))

    def above_copy(target):
        return remote(pre.at[target], abv, bs.at[target], br.at[0], (c, h, target))

    def arrive(k):
        for cc in range(C):
            @pl.when(c == cc)
            def _():
                here, there, left, right = tracer_copies(cc, k, cc)
                pl.when(k == cc)(here.wait)
                pl.when(k != cc)(there.wait_recv)
                pl.when(has_left)(left.wait_recv)
                pl.when(has_right)(right.wait_recv)

        @pl.loop(0, deep + 2)
        def _(l):
            T[0, k, l, pl.ds(rows, TILE)] = jnp.where(sub < TILE // 2, side[1, k, l], side[0, k, l])

    def optics(m):
        return (0.5 + m * m) / levels

    def light_totals():
        run = jnp.zeros((rows, cols), jnp.float32)
        for block in range(Z):
            pre[block] = run
            for l in range(group):
                run = run + optics(T[SUBSTEPS, 0, 1 + block * group + l, pl.ds(0, rows)])
        tot[...] = run
        for c2 in range(1, C):
            pl.when(c < c2)(total_copy(c2, c).start)

    def light_above():
        base = jnp.zeros((rows, cols), jnp.float32)
        abv[...] = base
        for c2 in range(C - 1):
            @pl.when(c > c2)
            def _():
                total_copy(c, c2).wait_recv()
                abv[...] += totr[c2]
        for block in range(1, Z):
            pre[block] = pre[block] + abv[...]
            above_copy(block).start()

    def work(index, carry):
        s, k = index // C, lax.rem(index, C)
        pl.when(s == 0)(functools.partial(arrive, k))

        @pl.when(s > 0)
        def _():
            down, up = halo(s, k)
            pl.when(c > 0)(down.wait_recv)
            pl.when(c < C - 1)(up.wait_recv)

        pl.when((s == SUBSTEPS - 1) & (k == C - 1) & (z == 0))(light_above)

        def level(l, carry):
            up, mid, down = T[s, k, l], T[s, k, l + 1], T[s, k, l + 2]
            T[s + 1, k, l + 1] = (
                W[0, l] * mid + W[1, l] * pltpu.roll(mid, 1, 0) + W[2, l] * pltpu.roll(mid, wide - 1, 0)
                + W[3, l] * pltpu.roll(mid, 1, 1) + W[4, l] * pltpu.roll(mid, cols - 1, 1)
                + CF[2, l + 1] * (down - mid) + CF[2, l] * (up - mid)
            )
            return carry

        lax.fori_loop(0, deep, level, 0, unroll=2)

        @pl.when(s < SUBSTEPS - 1)
        def _():
            down, up = halo(s + 1, k)
            pl.when(c < C - 1)(down.start)
            pl.when(c > 0)(up.start)

        @pl.when(s == SUBSTEPS - 1)
        def _():
            for d in range(1, Z):
                deliver(k, lax.rem(z + d, Z), z).start()
            F[k * Z + z] = T[SUBSTEPS, k, pl.ds(1 + z * group, group), pl.ds(0, rows)]
            pl.when((k == 0) & (z == 0))(light_totals)

        return carry

    lax.fori_loop(0, SUBSTEPS * C, work, 0)

    pl.when(z > 0)(above_copy(z).wait_recv)
    for k in range(C):
        for d in range(1, Z):
            deliver(k, z, lax.rem(z + d, Z)).wait_recv()

    def react_tile(index, carry):
        l, r = index // (rows // TILE), lax.rem(index, rows // TILE)
        here = pl.ds(pl.multiple_of(r * TILE, TILE), TILE)
        field = [F[j, l, here] for j in range(F.shape[0])]
        tau = optics(field[0])
        depth = abv[here]
        abv[here] = depth + tau
        light_top = sun[here] * jnp.exp(-depth)
        heat[l, here] = levels * light_top * (1.0 - jnp.exp(-tau))
        light_mid = light_top * jnp.exp(-0.5 * tau)
        limit = light_mid / (light_mid + HALF_LIGHT)
        for i in range(F.shape[0]):
            growth = react[i, 0] * field[0]
            for j in range(1, F.shape[0]):
                growth = growth + react[i, j] * field[j]
            out[i, l, here] = field[i] + limit * growth
        return carry

    lax.fori_loop(0, group * (rows // TILE), react_tile, 0)

    pl.when(has_left)(to_left.wait_send)
    pl.when(has_right)(to_right.wait_send)
    pl.when(z < Z - 1)(lambda: coef_copy(1, z).wait_send())
    pl.when(z > 0)(lambda: coef_copy(0, z).wait_send())
    for d in range(1, Z):
        pl.when((z >= d) & (z < Z - 1))(lambda: coef_copy(1, z - d).wait_send())
        pl.when((z + d < Z) & (z > 0))(lambda: coef_copy(0, z + d).wait_send())
    for c2 in range(C):
        here, there, left, right = tracer_copies(c2, c, c2)
        pl.when(c != c2)(there.wait_send)
        pl.when(has_right)(left.wait_send)
        pl.when(has_left)(right.wait_send)
    pl.when(c < C - 1)(kup.wait_send)
    for s in range(1, SUBSTEPS):
        for k in range(C):
            down, up = halo(s, k)
            pl.when(c < C - 1)(down.wait_send)
            pl.when(c > 0)(up.wait_send)
    for k in range(C):
        for d in range(1, Z):
            deliver(k, lax.rem(z + d, Z), z).wait_send()

    @pl.when(z == 0)
    def _():
        for c2 in range(1, C):
            pl.when(c < c2)(total_copy(c2, c).wait_send)
        for block in range(1, Z):
            above_copy(block).wait_send()


def per_device(dims, tracers, eastward, northward, surface_height, sea_mask, mixing, sunlight, reaction):
    C, H, Z, levels = dims
    group, rows, cols = eastward.shape
    wide, deep, f32 = rows + TILE, group * Z, jnp.float32
    dma = pltpu.SemaphoreType.DMA
    vmem = pl.BlockSpec(memory_space=pltpu.VMEM)
    plane = jax.ShapeDtypeStruct((group, rows, cols), f32)
    return pl.pallas_call(
        functools.partial(kernel, dims),
        out_shape=(
            plane, plane, jax.ShapeDtypeStruct((C * Z, group, rows, cols), f32), plane,
        ),
        in_specs=[pl.BlockSpec(memory_space=pltpu.HBM)] * 7 + [pl.BlockSpec(memory_space=pltpu.SMEM)],
        out_specs=(vmem,) * 4,
        scratch_shapes=[
            pltpu.VMEM((3 * group + 2, rows + 2 * TILE, cols), f32),
            pltpu.VMEM((rows, cols), jnp.int32), pltpu.VMEM((rows, cols), f32),
            pltpu.VMEM((SUBSTEPS + 1, C, deep + 2, wide, cols), f32),
            pltpu.VMEM((2, C, deep + 2, TILE, cols), f32),
            pltpu.VMEM((C * Z, group, rows, cols), f32),
            pltpu.VMEM((3, deep + 1, wide, cols), f32),
            pltpu.VMEM((5, deep, wide, cols), f32),
            pltpu.VMEM((rows, cols), f32),
            pltpu.VMEM((C, rows, cols), f32),
            pltpu.VMEM((Z, rows, cols), f32),
            pltpu.VMEM((rows, cols), f32),
            dma((6,)), dma((2,)), dma((2,)),
            dma((C, 3)), dma((1,)), dma((C, 3)),
            dma((2, Z)), dma((Z,)),
            dma((1,)), dma((1,)),
            dma((SUBSTEPS, C, 2)), dma((SUBSTEPS, C, 2)),
            dma((C, Z)), dma((C, Z)),
            dma((C,)), dma((C,)),
            dma((Z,)), dma((1,)),
        ],
        compiler_params=pltpu.CompilerParams(
            collective_id=0, has_side_effects=True, vmem_limit_bytes=63 * 1024 * 1024
        ),
    )(eastward, northward, mixing, surface_height, sea_mask, tracers, sunlight, reaction)


def solution(mesh):
    C, H, Z = (mesh.shape[a] for a in ("comp", "horiz", "trc"))

    def local(tracers, eastward, *rest):
        dims = (C, H, Z, eastward.shape[0] * C * Z)
        return per_device(dims, tracers, eastward, *rest)

    return jax.shard_map(
        local,
        mesh=mesh,
        in_specs=(
            P(("comp", "trc"), None, "horiz", None),
            P(("comp", "trc"), "horiz", None),
            P(("comp", "trc"), "horiz", None),
            P("horiz", None),
            P("horiz", None),
            P(("comp", "trc"), "horiz", None),
            P("horiz", None),
            P(),
        ),
        out_specs=(
            P(("comp", "trc"), "horiz", None),
            P(("comp", "trc"), "horiz", None),
            P(None, ("comp", "trc"), "horiz", None),
            P(("comp", "trc"), "horiz", None),
        ),
        check_vma=False,
    )
```
